32 devices in a mesh: row: 8 (over y, x, core), col: 4 (over z).
Axes of the slice: x: 2, y: 2, z: 4, core: 2. Of those that a mesh axis runs over, the one named last changes fastest.
Arguments:
- a_blocks: float32 [8, 8, 12, 128, 128], P('row', 'col'), may hold values from -0.5 to 0.5
- b_blocks: float32 [8, 4, 20, 128, 128], P('row', 'col'), may hold values from -5 to 5
- product_lists: int32 [8, 4, 8, 64, 3], P('row', 'col'), may hold values from 0 to 48, as said below
Outputs:
- c_blocks: float32 [8, 4, 48, 128, 128], P('row', 'col')
The draws below stay inside these ranges and needn't reach their ends.
Inputs may be any that keep to these rules, and one draw needn't show every extreme that they name: `product_lists`: entry 0 of a product is a slot of the A panel, entry 1 a slot of the B panel, entry 2 a slot of the C panel or 48 for padding. In every list the real products come first, at least 21 of them; some lists of every draw have no padding.
All inputs are finite; a program needn't handle non-finite values.
Results may differ from the reference program's by a relative error of at most 0.0003.
Values sent between devices are 32-bit elements; how exact they have to be, the bound alone decides.
No kernel may reach another device: no remote copies, remote signals or barrier semaphores. Data moves between devices by JAX's collectives and lax.ppermute only.
A program may use at most 128 MiB of HBM per device.

```python
import jax
import jax.numpy as jnp
from jax import lax

BS = 128
SA = 12
SB = 20
SC = 48
P_SIZE = 64
N_ROW = 8
N_COL = 4


def draw_product_lists(key, part):
    key_left, key_right, key_out, key_count = jax.random.split(jax.random.fold_in(key, 17), 4)
    shape = (N_ROW, N_COL, N_ROW, P_SIZE)
    left_slot = jax.random.randint(key_left, shape, 0, SA, dtype=jnp.int32)
    right_slot = jax.random.randint(key_right, shape, 0, SB, dtype=jnp.int32)
    out_slot = jax.random.randint(key_out, shape, 0, SC, dtype=jnp.int32)
    counts = jax.random.randint(key_count, (N_ROW, N_COL, N_ROW, 1), P_SIZE // 3, P_SIZE + P_SIZE // 4, dtype=jnp.int32)
    counts = jnp.minimum(counts, P_SIZE)
    position = jnp.arange(P_SIZE, dtype=jnp.int32)
    out_slot = jnp.where(position < counts, out_slot, SC)
    return jnp.stack([left_slot, right_slot, out_slot], axis=-1).astype(jnp.int32)


def levels(own_key, shape, cuts, smallest, largest):
    gain, own = 1.0, jax.random.fold_in(own_key, 6)
    for dim, parts in cuts:
        heights = jnp.exp(jax.random.uniform(jax.random.fold_in(own, dim), (parts,), jnp.float32, smallest / len(cuts), largest / len(cuts)))
        gain = gain * jnp.repeat(heights, shape[dim] // parts).reshape([-1 if axis == dim else 1 for axis in range(len(shape))])
    return gain


def scatter_about(own_key, extent, spread, limit, cuts=(), kind=jnp.bfloat16):
    array = jax.random.normal(own_key, extent, jnp.float32) * spread
    if len(cuts) > 0:
        array = levels(own_key, extent, cuts, -0.22, 0.18) * array
    return jnp.clip(array, min=-limit, max=limit).astype(kind)


def setup_inputs(seed: int = 0) -> dict:
    splits = jax.random.split(jax.random.key(seed), 4)
    return {
        "a_blocks": scatter_about(splits[0], (N_ROW, N_ROW, SA, BS, BS), BS ** -0.5, 0.5, ((0, 8), (1, 4)), jnp.float32),
        "b_blocks": scatter_about(splits[1], (N_ROW, N_COL, SB, BS, BS), ((SC / (0.7 * N_ROW * P_SIZE)) ** 0.5), 5.0, ((0, 8), (1, 4)), jnp.float32),
        "product_lists": draw_product_lists(jax.random.fold_in(splits[3], 71), 0),
    }


def reference(a_blocks, b_blocks, product_lists):
    def device(index):
        row_index = index // N_COL
        col_index = index % N_COL

        def turn(panel, totals):
            left = a_blocks[row_index, panel]
            right = b_blocks[panel, col_index]
            entries = product_lists[row_index, col_index, panel]
            left_sel = jnp.take(left, entries[:, 0], axis=0).astype(jnp.float32)
            right_sel = jnp.take(right, entries[:, 1], axis=0).astype(jnp.float32)
            terms = jnp.einsum("pij,pjk->pik", left_sel, right_sel, precision=lax.Precision.HIGHEST)
            summed = jax.ops.segment_sum(terms, entries[:, 2], SC + 1)
            return totals + summed[:SC]

        start = jnp.zeros((SC, BS, BS), jnp.float32)
        return lax.fori_loop(0, N_ROW, turn, start)

    result = lax.map(device, jnp.arange(N_ROW * N_COL, dtype=jnp.int32))
    return result.reshape(N_ROW, N_COL, SC, BS, BS)
```

```python
import functools

import jax
import jax.numpy as jnp
from jax import lax
from jax.experimental import pallas as pl
from jax.experimental.pallas import tpu as pltpu
from jax.sharding import PartitionSpec as P

SC = 48
GROUP = 16
F32, BF16 = jnp.float32, jnp.bfloat16


def along(value, axis, pairs):
    return lax.ppermute(value, axis, pairs)


def rows_by_distance(own, count):
    half = own.shape[0] // 2
    swap = lambda v, bit: along(v, "row", [(i, i ^ bit) for i in range(count)])
    held = {0: [own]}
    bits = [1 << i for i in range(count.bit_length()) if 1 < (1 << i) < count]
    whole = {0: own}
    for bit in bits:
        whole[bit] = swap(own, bit)
        held[bit] = [whole[bit]]
    halves = {m: (whole[m][:half], whole[m][half:]) for m in whole}
    for mask in range(2, count, 2):
        if mask in halves:
            continue
        low, high = mask & -mask, 1 << (mask.bit_length() - 1)
        halves[mask] = (swap(halves[mask ^ high][0], high), swap(halves[mask ^ low][1], low))
        held[mask] = list(halves[mask])
    for mask in list(held):
        held[mask | 1] = [swap(piece, 1) for piece in held[mask]]
    return [held[mask] for mask in range(count)]


def split(x):
    high = x.astype(BF16)
    return high, (x - high.astype(F32)).astype(BF16)


def product(left, right):
    both = jnp.dot(left, jnp.concatenate([right, right], 0), preferred_element_type=F32)
    n = both.shape[1] // 2
    return both[:, :n] + both[:, n:]


def split_into(source, target, base):
    n = source.shape[-1]

    @pl.loop(0, source.shape[0])
    def _(i):
        high, low = split(source[i])
        target[base + i, :, :n] = high
        target[base + i, :, n:] = low


def add_products(meta, lists, a_split, b_split, acc, sources, a_slots, b_slots, per_list, b_base):
    @pl.loop(0, sources)
    def _(t):
        panel, count = meta[3 * t], meta[3 * t + 1]
        b_at = b_base(t) * b_slots

        @pl.loop(0, (count + GROUP - 1) // GROUP)
        def _(g):
            terms, slots = [], []
            for u in range(GROUP):
                entry = lists[panel * per_list + g * GROUP + u]
                slots.append(entry & 1023)
                right = b_split[b_at + ((entry >> 10) & 1023)]
                left = a_split[t * a_slots + (entry >> 20)]
                terms.append(product(left, right))
            for slot, term in zip(slots, terms):
                acc[slot] += term


def first_kernel(sources, pieces, per_list, *refs):
    meta, lists = refs[:2]
    a_refs = refs[2 : 2 + sources]
    b_refs = refs[2 + sources : 2 + sources + len(pieces)]
    acc_out, b_out, a_buf, b_buf, a_split, b_split, acc, sem = refs[2 + sources + len(pieces) :]
    a_slots = a_refs[0].shape[0]
    b_slots = b_split.shape[0] // (1 + max(code for code, _ in pieces))
    copies = []
    for t in range(sources):
        copies.append((pltpu.make_async_copy(a_refs[t], a_buf.at[pl.ds(t * a_slots, a_slots)], sem.at[t]), t * a_slots, a_slots))
    b_copies = []
    for j, (code, offset) in enumerate(pieces):
        n, at = b_refs[j].shape[0], code * b_slots + offset
        b_copies.append((pltpu.make_async_copy(b_refs[j], b_buf.at[pl.ds(at, n)], sem.at[sources + j]), at, n))
    for copy, _, _ in copies + b_copies:
        copy.start()
    acc[...] = jnp.zeros_like(acc)
    for copy, at, n in copies:
        copy.wait()
        split_into(a_buf.at[pl.ds(at, n)], a_split, at)
    for copy, at, n in b_copies:
        copy.wait()
        split_into(b_buf.at[pl.ds(at, n)], b_split, at)
    keep = pltpu.make_async_copy(b_split, b_out, sem.at[0])
    keep.start()
    add_products(
        meta, lists, a_split, b_split, acc, sources, a_slots, b_slots, per_list, lambda t: meta[3 * t + 2]
    )
    done = pltpu.make_async_copy(acc.at[pl.ds(0, SC)], acc_out, sem.at[1])
    done.start()
    keep.wait()
    done.wait()


def later_kernel(sources, per_list, *refs):
    meta, lists = refs[:2]
    a_refs = refs[2 : 2 + sources]
    b_in, acc_in, acc_out, a_buf, a_split, b_split, acc, sem = refs[2 + sources :]
    a_slots = a_refs[0].shape[0]
    b_slots = b_split.shape[0] // sources
    load = pltpu.make_async_copy(acc_in, acc.at[pl.ds(0, SC)], sem.at[0])
    load.start()

    def copies(t):
        b_at = meta[3 * t + 2] * b_slots
        return (
            pltpu.make_async_copy(a_refs[t], a_buf.at[pl.ds(t * a_slots, a_slots)], sem.at[1 + 2 * t]),
            pltpu.make_async_copy(
                b_in.at[pl.ds(b_at, b_slots)], b_split.at[pl.ds(t * b_slots, b_slots)], sem.at[2 + 2 * t]
            ),
        )

    for t in range(sources):

        @pl.when(meta[3 * t + 1] > 0)
        def _():
            for copy in copies(t):
                copy.start()

    for t in range(sources):

        @pl.when(meta[3 * t + 1] > 0)
        def _():
            a_copy, b_copy = copies(t)
            a_copy.wait()
            split_into(a_buf.at[pl.ds(t * a_slots, a_slots)], a_split, t * a_slots)
            b_copy.wait()

    load.wait()
    add_products(meta, lists, a_split, b_split, acc, sources, a_slots, b_slots, per_list, lambda t: t)
    done = pltpu.make_async_copy(acc.at[pl.ds(0, SC)], acc_out, sem.at[0])
    done.start()
    done.wait()


ANY = pl.BlockSpec(memory_space=pl.ANY)
SMEM = pl.BlockSpec(memory_space=pltpu.SMEM)


def run_first(meta, lists, a_list, b_held, per_list):
    a_slots, size, _ = a_list[0].shape
    sources, codes = len(a_list), len(b_held)
    b_slots = sum(piece.shape[0] for piece in b_held[0])
    pieces, arrays = [], []
    for code, parts in enumerate(b_held):
        offset = 0
        for part in parts:
            pieces.append((code, offset))
            arrays.append(part)
            offset += part.shape[0]
    work = sources * per_list * 2 * size**3 * 4
    return pl.pallas_call(
        functools.partial(first_kernel, sources, tuple(pieces), per_list),
        out_shape=(
            jax.ShapeDtypeStruct((SC, size, size), F32),
            jax.ShapeDtypeStruct((codes * b_slots, size, 2 * size), BF16),
        ),
        in_specs=[SMEM, SMEM] + [ANY] * (sources + len(arrays)),
        out_specs=(ANY, ANY),
        scratch_shapes=[
            pltpu.VMEM((sources * a_slots, size, size), F32),
            pltpu.VMEM((codes * b_slots, size, size), F32),
            pltpu.VMEM((sources * a_slots, size, 2 * size), BF16),
            pltpu.VMEM((codes * b_slots, size, 2 * size), BF16),
            pltpu.VMEM((SC + 1, size, size), F32),
            pltpu.SemaphoreType.DMA((sources + len(arrays),)),
        ],
        compiler_params=pltpu.CompilerParams(vmem_limit_bytes=56 << 20),
        cost_estimate=pl.CostEstimate(flops=work, bytes_accessed=40 << 20, transcendentals=0),
        name="first_panels",
    )(meta, lists, *a_list, *arrays)


def run_later(meta, lists, a_list, b_all, acc, codes, per_list):
    a_slots, size, _ = a_list[0].shape
    sources = len(a_list)
    b_slots = b_all.shape[0] // codes
    work = per_list * 2 * size**3 * 4 * sources // 2
    return pl.pallas_call(
        functools.partial(later_kernel, sources, per_list),
        out_shape=jax.ShapeDtypeStruct(acc.shape, F32),
        in_specs=[SMEM, SMEM] + [ANY] * (sources + 2),
        out_specs=ANY,
        scratch_shapes=[
            pltpu.VMEM((sources * a_slots, size, size), F32),
            pltpu.VMEM((sources * a_slots, size, 2 * size), BF16),
            pltpu.VMEM((sources * b_slots, size, 2 * size), BF16),
            pltpu.VMEM((SC + 1, size, size), F32),
            pltpu.SemaphoreType.DMA((1 + 2 * sources,)),
        ],
        compiler_params=pltpu.CompilerParams(vmem_limit_bytes=24 << 20),
        cost_estimate=pl.CostEstimate(flops=work, bytes_accessed=16 << 20, transcendentals=0),
        name="later_panels",
    )(meta, lists, *a_list, b_all, acc)


def on_device(cols, rows, a_blocks, b_blocks, product_lists):
    row, col = lax.axis_index("row"), lax.axis_index("col")
    own = a_blocks[0]
    per_device = own.shape[0]
    entries = product_lists[0, 0]
    per_list = -(-entries.shape[1] // GROUP) * GROUP
    entries = jnp.pad(entries, ((0, 0), (0, per_list - entries.shape[1]), (0, 0)), constant_values=SC)
    real = entries[:, :, 2] < SC
    counts = jnp.sum(real.astype(jnp.int32), axis=1)
    packed = jnp.where(real, (entries[:, :, 0] << 20) | (entries[:, :, 1] << 10) | entries[:, :, 2], SC)
    packed = packed.reshape(-1)

    def meta_of(sources):
        out = []
        for holder, q in sources:
            valid = (holder >= 0) & (holder < cols)
            panel = jnp.where(valid, holder * per_device + q, 0)
            count = jnp.where(valid, lax.dynamic_index_in_dim(counts, panel, 0, keepdims=False), 0)
            out += [panel, count, panel ^ row]
        return jnp.stack(out).astype(jnp.int32)

    arrived = []
    for q in range(per_device):
        right = left = own[q]
        steps = [[(own[q], (col, q))]]
        for s in range(1, cols):
            right = along(right, "col", [(i, i + 1) for i in range(s - 1, cols - 1)])
            left = along(left, "col", [(i, i - 1) for i in range(1, cols - s + 1)])
            steps.append([(right, (col - s, q)), (left, (col + s, q))])
        arrived.append(steps)

    b_held = rows_by_distance(b_blocks[0, 0], rows)

    early = [item for s in range(min(2, cols)) for q in range(per_device) for item in arrived[q][s]]
    acc, b_all = run_first(meta_of([m for _, m in early]), packed, [a for a, _ in early], b_held, per_list)
    for s in range(2, cols):
        if s < cols - 1:
            stages = [[item for q in range(per_device) for item in arrived[q][s]]]
        else:
            stages = [arrived[q][s] for q in range(per_device)]
        for items in stages:
            acc = run_later(
                meta_of([m for _, m in items]), packed, [a for a, _ in items], b_all, acc, rows, per_list
            )
    return acc.reshape((1, 1) + acc.shape)


def solution(mesh):
    spec = P("row", "col", None, None, None)
    return jax.shard_map(
        functools.partial(on_device, mesh.shape["col"], mesh.shape["row"]),
        mesh=mesh,
        in_specs=(spec, spec, spec),
        out_specs=spec,
        check_vma=False,
    )
```

```python
import functools

import jax
import jax.numpy as jnp
from jax import lax
from jax.experimental import pallas as pl
from jax.experimental.pallas import tpu as pltpu
from jax.sharding import PartitionSpec as P

SC = 48
GROUP = 32
F32, BF16 = jnp.float32, jnp.bfloat16
ANY = pl.BlockSpec(memory_space=pl.ANY)
SMEM = pl.BlockSpec(memory_space=pltpu.SMEM)
VMEM = pl.BlockSpec(memory_space=pltpu.VMEM)
SHORT = pl.CostEstimate(flops=1 << 16, bytes_accessed=1 << 16, transcendentals=0)


def together(*values):
    return lax.optimization_barrier(values)


def in_hbm(x):
    return pltpu.with_memory_space_constraint(x, pltpu.HBM)


def in_vmem(x):
    return pltpu.with_memory_space_constraint(x, pltpu.VMEM)


def rest_of_rows(held, half, rows, swap):
    halves = {code: (parts[0][:half], parts[0][half:]) for code, parts in held.items()}
    for code in range(2, rows, 2):
        if code not in held:
            low, high = code & -code, 1 << (code.bit_length() - 1)
            halves[code] = (swap(halves[code ^ high][0], high), swap(halves[code ^ low][1], low))
            held[code] = list(halves[code])


def split(x):
    high = x.astype(BF16)
    return high, (x - high.astype(F32)).astype(BF16)


def product(left, right):
    both = jnp.dot(left, jnp.concatenate([right, right], 0), preferred_element_type=F32)
    n = both.shape[1] // 2
    return both[:, :n] + both[:, n:]


def split_into(source, target):
    n = source.shape[-1]

    @pl.loop(0, source.shape[0])
    def _(i):
        high, low = split(source[i])
        target[i, :, :n] = high
        target[i, :, n:] = low


def panel_at(info, cols, per_device, step, q):
    col = info[1]
    holder = col + step * (1 - 2 * (col & 1))
    valid = (holder >= 0) & (holder < cols)
    panel = jnp.where(valid, holder * per_device + q, 0)
    return panel, jnp.where(valid, info[2 + panel], 0)


def add_list(info, lists_at, per_list, panel, count, a_split, b_split, acc):
    @pl.loop(0, (count + GROUP - 1) // GROUP)
    def _(g):
        terms, slots = [], []
        for u in range(GROUP):
            entry = info[lists_at + panel * per_list + g * GROUP + u]
            slots.append(entry & 1023)
            terms.append(product(a_split[entry >> 20], b_split[(entry >> 10) & 1023]))
        for slot, term in zip(slots, terms):
            acc[slot] += term


def panel_kernel(sizes, per_list, steps, ahead, pieces, first, info, *refs):
    cols, rows, per_device = sizes
    sources = 1 + max(step[0] for step in steps)
    a_refs, b_refs = refs[:sources], refs[sources : sources + len(pieces)]
    acc, *refs = refs[sources + len(pieces) + (not first) :]
    readies, refs = refs[: len(ahead)], refs[len(ahead) :]
    a_buf, b_buf, a_split, b_split, a_sem, b_sem = refs
    row, lists_at = info[0], 2 + rows

    def fetch(t, panel, count):
        for (code, at), b_ref in zip(pieces, b_refs):

            @pl.when((count > 0) & (code == (panel ^ row)))
            def _():
                pltpu.make_async_copy(b_ref, b_buf.at[t, pl.ds(at, b_ref.shape[0])], b_sem.at[t]).start()

    def fetched(t):
        return pltpu.make_async_copy(b_buf.at[t], b_buf.at[t], b_sem.at[t])

    found = [panel_at(info, cols, per_device, step, q) for _, _, step, q in steps]
    found += [panel_at(info, cols, per_device, step, q) for step, q in ahead]
    for t, (panel, count) in enumerate(found):
        fetch(t, panel, count)
        if t < len(steps):
            a_ref = a_refs[steps[t][0]].at[steps[t][1]]

            @pl.when(count > 0)
            def _():
                pltpu.make_async_copy(a_ref, a_buf.at[t], a_sem.at[t]).start()

    if first:
        acc[...] = jnp.zeros_like(acc)
    for t in range(len(steps)):
        panel, count = found[t]
        a_ref = a_refs[steps[t][0]].at[steps[t][1]]

        @pl.when(count > 0)
        def _():
            pltpu.make_async_copy(a_ref, a_buf.at[t], a_sem.at[t]).wait()
            split_into(a_buf.at[t], a_split)
            fetched(t).wait()
            split_into(b_buf.at[t], b_split)

        add_list(info, lists_at, per_list, panel, count, a_split, b_split, acc)
    for j, ready in enumerate(readies):
        t = len(steps) + j

        @pl.when(found[t][1] > 0)
        def _():
            fetched(t).wait()
            split_into(b_buf.at[t], ready)


def ready_kernel(sizes, per_list, step, q, last, info, a_ref, b_split, _, acc, *refs):
    if last:
        out, *refs = refs
    a_split, out_sem = refs
    panel, count = panel_at(info, sizes[0], sizes[2], step, q)

    @pl.when(count > 0)
    def _():
        split_into(a_ref, a_split)

    add_list(info, 2 + sizes[1], per_list, panel, count, a_split, b_split, acc)
    if last:
        done = pltpu.make_async_copy(acc.at[pl.ds(0, SC)], out, out_sem)
        done.start()
        done.wait()


def add_panels(sizes, per_list, info, items, b_held, acc, ahead):
    _, a_slots, size, _ = items[0][0].shape
    steps = tuple((i, j, step, q + j) for i, (a, step, q) in enumerate(items) for j in range(a.shape[0]))
    a_list = [in_hbm(a) for a, _, _ in items]
    b_slots = sum(piece.shape[0] for piece in b_held[0])
    pieces, b_list = [], []
    for code, parts in enumerate(b_held):
        offset = 0
        for part in parts:
            pieces.append((code, offset))
            b_list.append(in_hbm(part))
            offset += part.shape[0]
    count = len(steps) + len(ahead)
    ready = jax.ShapeDtypeStruct((b_slots, size, 2 * size), BF16)
    first = acc is None
    return pl.pallas_call(
        functools.partial(panel_kernel, sizes, per_list, steps, tuple(ahead), tuple(pieces), first),
        out_shape=[jax.ShapeDtypeStruct((SC + 1, size, size), F32)] + [ready] * len(ahead),
        in_specs=[SMEM] + [ANY] * (len(a_list) + len(b_list)) + ([] if first else [VMEM]),
        out_specs=[VMEM] * (1 + len(ahead)),
        input_output_aliases={} if first else {1 + len(a_list) + len(b_list): 0},
        scratch_shapes=[
            pltpu.VMEM((len(steps), a_slots, size, size), F32),
            pltpu.VMEM((count, b_slots, size, size), F32),
            pltpu.VMEM((a_slots, size, 2 * size), BF16),
            pltpu.VMEM((b_slots, size, 2 * size), BF16),
            pltpu.SemaphoreType.DMA((len(steps),)),
            pltpu.SemaphoreType.DMA((count,)),
        ],
        compiler_params=pltpu.CompilerParams(vmem_limit_bytes=24 << 20),
        cost_estimate=SHORT,
        name="add_panels",
    )(info, *a_list, *b_list, *([] if first else [acc]))


def add_ready(sizes, per_list, info, a, step, q, b_ready, acc, last):
    a_slots, size, _ = a.shape
    out = [jax.ShapeDtypeStruct(acc.shape, F32)]
    if last:
        out.append(jax.ShapeDtypeStruct((SC, size, size), F32))
    return pl.pallas_call(
        functools.partial(ready_kernel, sizes, per_list, step, q, last),
        out_shape=out,
        in_specs=[SMEM, VMEM, VMEM, VMEM],
        out_specs=[VMEM, ANY][: len(out)],
        input_output_aliases={3: 0},
        scratch_shapes=[pltpu.VMEM((a_slots, size, 2 * size), BF16), pltpu.SemaphoreType.DMA],
        compiler_params=pltpu.CompilerParams(vmem_limit_bytes=16 << 20),
        cost_estimate=SHORT,
        name="add_last",
    )(info, in_vmem(a), b_ready, acc)[-1]


def on_device(cols, rows, a_blocks, b_blocks, product_lists):
    own, b_own = a_blocks[0], b_blocks[0, 0]
    per_device = own.shape[0]
    sizes = (cols, rows, per_device)
    entries = product_lists[0, 0]
    per_list = -(-entries.shape[1] // GROUP) * GROUP
    entries = jnp.pad(entries, ((0, 0), (0, per_list - entries.shape[1]), (0, 0)), constant_values=SC)
    real = entries[:, :, 2] < SC
    packed = jnp.where(real, (entries[:, :, 0] << 20) | (entries[:, :, 1] << 10) | entries[:, :, 2], SC)
    counts = jnp.sum(real.astype(jnp.int32), axis=1)
    place = jnp.stack([lax.axis_index("row"), lax.axis_index("col")]).astype(jnp.int32)
    info = jnp.concatenate([place, counts, packed.reshape(-1)])

    def over_even(value):
        return lax.ppermute(value, "col", [(i, i ^ 1) for i in range(cols) if i ^ 1 < cols])

    def over_odd(value):
        return lax.ppermute(value, "col", [(i, j) for i in range(cols) for j in [((i + 1) ^ 1) - 1] if 0 <= j < cols])

    def swap(value, bit):
        return lax.ppermute(value, "row", [(i, i ^ bit) for i in range(rows)])

    half = b_own.shape[0] // 2
    bits = [1 << i for i in range(1, rows.bit_length()) if (1 << i) < rows]
    x, y = over_even(own), over_odd(own)
    b_held = {0: [b_own]}
    b_held.update({bit: [swap(b_own, bit)] for bit in bits})
    stages = [[(own, 0, 0), (x, 1, 0), (y, -1, 0)]]

    even, odd = [x[q] for q in range(per_device)], y
    for s in range(2, cols):
        hop, other = (over_odd, over_even) if s % 2 == 0 else (over_even, over_odd)
        even = [hop(piece) for piece in even]
        if s < cols - 1:
            odd = other(odd)
            near_even = 1 if s % 2 else -1
            stages.append([(piece[None], near_even * s, q) for q, piece in enumerate(even)] + [(odd, -near_even * s, 0)])
        if s == 2:
            even[0], near = together(even[0], [b_held[bit] for bit in bits])
            b_held.update(zip(bits, near))
            rest_of_rows(b_held, half, rows, swap)
        if s == 3:
            stages[0][0] = (together(own, stages[1][-1][0])[0], 0, 0)
    b_held.update({code | 1: [swap(piece, 1) for piece in b_held[code]] for code in range(0, rows, 2)})
    b_held = [b_held[code] for code in range(rows)]
    acc, readies = None, []
    for i, items in enumerate(stages):
        ahead = [(cols - 1, q) for q in range(per_device)] if i == len(stages) - 1 else []
        acc, *readies = add_panels(sizes, per_list, info, items, b_held, acc, ahead)
    for q, piece in enumerate(even):
        acc = add_ready(sizes, per_list, info, piece, cols - 1, q, readies[q], acc, q == per_device - 1)
    return acc.reshape((1, 1) + acc.shape)


def solution(mesh):
    spec = P("row", "col", None, None, None)
    return jax.shard_map(
        functools.partial(on_device, mesh.shape["col"], mesh.shape["row"]),
        mesh=mesh,
        in_specs=(spec, spec, spec),
        out_specs=spec,
        check_vma=False,
    )
```

```python
import functools

import jax
import jax.numpy as jnp
from jax import lax
from jax.experimental import pallas as pl
from jax.experimental.pallas import tpu as pltpu
from jax.sharding import PartitionSpec as P

SC = 48
GROUP = 32
F32, BF16 = jnp.float32, jnp.bfloat16
ANY = pl.BlockSpec(memory_space=pl.ANY)
SMEM = pl.BlockSpec(memory_space=pltpu.SMEM)
VMEM = pl.BlockSpec(memory_space=pltpu.VMEM)
SHORT = pl.CostEstimate(flops=1 << 16, bytes_accessed=1 << 16, transcendentals=0)


def together(*values):
    return lax.optimization_barrier(values)


def in_hbm(x):
    return pltpu.with_memory_space_constraint(x, pltpu.HBM)


def in_vmem(x):
    return pltpu.with_memory_space_constraint(x, pltpu.VMEM)


def rest_of_rows(held, half, rows, swap):
    halves = {code: (parts[0][:half], parts[0][half:]) for code, parts in held.items()}
    for code in range(2, rows, 2):
        if code not in held:
            low, high = code & -code, 1 << (code.bit_length() - 1)
            halves[code] = (swap(halves[code ^ high][0], high), swap(halves[code ^ low][1], low))
            held[code] = list(halves[code])


def split(x):
    high = x.astype(BF16)
    return high, (x - high.astype(F32)).astype(BF16)


def product(left, right):
    both = jnp.dot(left, jnp.concatenate([right, right], 0), preferred_element_type=F32)
    n = both.shape[1] // 2
    return both[:, :n] + both[:, n:]


def split_into(source, target):
    n = source.shape[-1]

    @pl.loop(0, source.shape[0])
    def _(i):
        high, low = split(source[i])
        target[i, :, :n] = high
        target[i, :, n:] = low


def panel_at(info, cols, per_device, step, q):
    col = info[1]
    holder = col + step * (1 - 2 * (col & 1))
    valid = (holder >= 0) & (holder < cols)
    panel = jnp.where(valid, holder * per_device + q, 0)
    return panel, jnp.where(valid, info[2 + panel], 0)


def add_list(info, lists_at, per_list, panel, count, a_split, b_split, acc):
    @pl.loop(0, (count + GROUP - 1) // GROUP)
    def _(g):
        terms, slots = [], []
        for u in range(GROUP):
            entry = info[lists_at + panel * per_list + g * GROUP + u]
            slots.append(entry & 1023)
            terms.append(product(a_split[entry >> 20], b_split[(entry >> 10) & 1023]))
        for slot, term in zip(slots, terms):
            acc[slot] += term


def panel_kernel(sizes, per_list, steps, ahead, pieces, first, info, *refs):
    cols, rows, per_device = sizes
    sources = 1 + max(step[0] for step in steps)
    a_refs, b_refs = refs[:sources], refs[sources : sources + len(pieces)]
    acc, *refs = refs[sources + len(pieces) + (not first) :]
    readies, refs = refs[: len(ahead)], refs[len(ahead) :]
    a_buf, b_buf, a_split, b_split, a_sem, b_sem = refs
    row, lists_at = info[0], 2 + rows

    def fetch(t, panel, count):
        for (code, at), b_ref in zip(pieces, b_refs):

            @pl.when((count > 0) & (code == (panel ^ row)))
            def _():
                pltpu.make_async_copy(b_ref, b_buf.at[t, pl.ds(at, b_ref.shape[0])], b_sem.at[t]).start()

    def fetched(t):
        return pltpu.make_async_copy(b_buf.at[t], b_buf.at[t], b_sem.at[t])

    found = [panel_at(info, cols, per_device, step, q) for _, _, step, q in steps]
    found += [panel_at(info, cols, per_device, step, q) for step, q in ahead]
    for t, (panel, count) in enumerate(found):
        fetch(t, panel, count)
        if t < len(steps):
            a_ref = a_refs[steps[t][0]].at[steps[t][1]]

            @pl.when(count > 0)
            def _():
                pltpu.make_async_copy(a_ref, a_buf.at[t], a_sem.at[t]).start()

    if first:
        acc[...] = jnp.zeros_like(acc)
    for t in range(len(steps)):
        panel, count = found[t]
        a_ref = a_refs[steps[t][0]].at[steps[t][1]]

        @pl.when(count > 0)
        def _():
            pltpu.make_async_copy(a_ref, a_buf.at[t], a_sem.at[t]).wait()
            split_into(a_buf.at[t], a_split)
            fetched(t).wait()
            split_into(b_buf.at[t], b_split)

        add_list(info, lists_at, per_list, panel, count, a_split, b_split, acc)
    for j, ready in enumerate(readies):
        t = len(steps) + j

        @pl.when(found[t][1] > 0)
        def _():
            fetched(t).wait()
            split_into(b_buf.at[t], ready)


def ready_kernel(sizes, per_list, step, q, last, info, a_ref, b_split, _, acc, *refs):
    if last:
        out, *refs = refs
    a_split, out_sem = refs
    panel, count = panel_at(info, sizes[0], sizes[2], step, q)

    @pl.when(count > 0)
    def _():
        split_into(a_ref, a_split)

    add_list(info, 2 + sizes[1], per_list, panel, count, a_split, b_split, acc)
    if last:
        done = pltpu.make_async_copy(acc.at[pl.ds(0, SC)], out, out_sem)
        done.start()
        done.wait()


def add_panels(sizes, per_list, info, items, b_held, acc, ahead):
    _, a_slots, size, _ = items[0][0].shape
    steps = tuple((i, j, step, q + j) for i, (a, step, q) in enumerate(items) for j in range(a.shape[0]))
    a_list = [in_hbm(a) if i != 1 else a for i, (a, _, _) in enumerate(items)]
    b_slots = sum(piece.shape[0] for piece in b_held[0])
    pieces, b_list = [], []
    for code, parts in enumerate(b_held):
        offset = 0
        for part in parts:
            pieces.append((code, offset))
            b_list.append(in_hbm(part))
            offset += part.shape[0]
    count = len(steps) + len(ahead)
    ready = jax.ShapeDtypeStruct((b_slots, size, 2 * size), BF16)
    first = acc is None
    return pl.pallas_call(
        functools.partial(panel_kernel, sizes, per_list, steps, tuple(ahead), tuple(pieces), first),
        out_shape=[jax.ShapeDtypeStruct((SC + 1, size, size), F32)] + [ready] * len(ahead),
        in_specs=[SMEM] + [ANY] * (len(a_list) + len(b_list)) + ([] if first else [VMEM]),
        out_specs=[VMEM] * (1 + len(ahead)),
        input_output_aliases={} if first else {1 + len(a_list) + len(b_list): 0},
        scratch_shapes=[
            pltpu.VMEM((len(steps), a_slots, size, size), F32),
            pltpu.VMEM((count, b_slots, size, size), F32),
            pltpu.VMEM((a_slots, size, 2 * size), BF16),
            pltpu.VMEM((b_slots, size, 2 * size), BF16),
            pltpu.SemaphoreType.DMA((len(steps),)),
            pltpu.SemaphoreType.DMA((count,)),
        ],
        compiler_params=pltpu.CompilerParams(vmem_limit_bytes=24 << 20),
        cost_estimate=SHORT,
        name="add_panels",
    )(info, *a_list, *b_list, *([] if first else [acc]))


def add_ready(sizes, per_list, info, a, step, q, b_ready, acc, last):
    a_slots, size, _ = a.shape
    out = [jax.ShapeDtypeStruct(acc.shape, F32)]
    if last:
        out.append(jax.ShapeDtypeStruct((SC, size, size), F32))
    return pl.pallas_call(
        functools.partial(ready_kernel, sizes, per_list, step, q, last),
        out_shape=out,
        in_specs=[SMEM, VMEM, VMEM, VMEM],
        out_specs=[VMEM, ANY][: len(out)],
        input_output_aliases={3: 0},
        scratch_shapes=[pltpu.VMEM((a_slots, size, 2 * size), BF16), pltpu.SemaphoreType.DMA],
        compiler_params=pltpu.CompilerParams(vmem_limit_bytes=16 << 20),
        cost_estimate=SHORT,
        name="add_last",
    )(info, in_vmem(a), b_ready, acc)[-1]


def on_device(cols, rows, a_blocks, b_blocks, product_lists):
    own, b_own = a_blocks[0], b_blocks[0, 0]
    per_device = own.shape[0]
    sizes = (cols, rows, per_device)
    entries = product_lists[0, 0]
    per_list = -(-entries.shape[1] // GROUP) * GROUP
    entries = jnp.pad(entries, ((0, 0), (0, per_list - entries.shape[1]), (0, 0)), constant_values=SC)
    real = entries[:, :, 2] < SC
    packed = jnp.where(real, (entries[:, :, 0] << 20) | (entries[:, :, 1] << 10) | entries[:, :, 2], SC)
    counts = jnp.sum(real.astype(jnp.int32), axis=1)
    place = jnp.stack([lax.axis_index("row"), lax.axis_index("col")]).astype(jnp.int32)
    info = jnp.concatenate([place, counts, packed.reshape(-1)])

    def over_even(value):
        return lax.ppermute(value, "col", [(i, i ^ 1) for i in range(cols) if i ^ 1 < cols])

    def over_odd(value):
        return lax.ppermute(value, "col", [(i, j) for i in range(cols) for j in [((i + 1) ^ 1) - 1] if 0 <= j < cols])

    def swap(value, bit):
        return lax.ppermute(value, "row", [(i, i ^ bit) for i in range(rows)])

    half = b_own.shape[0] // 2
    bits = [1 << i for i in range(1, rows.bit_length()) if (1 << i) < rows]
    x, y = over_even(own), over_odd(own)
    b_held = {0: [b_own]}
    b_held.update({bit: [swap(b_own, bit)] for bit in bits})
    stages = [[(own, 0, 0), (x, 1, 0), (y, -1, 0)]]

    even, odd = [x[q] for q in range(per_device)], y
    for s in range(2, cols):
        hop, other = (over_odd, over_even) if s % 2 == 0 else (over_even, over_odd)
        even = [hop(piece) for piece in even]
        if s < cols - 1:
            odd = other(odd)
            near_even = 1 if s % 2 else -1
            stages.append([(piece[None], near_even * s, q) for q, piece in enumerate(even)] + [(odd, -near_even * s, 0)])
        if s == 2:
            even[0], near = together(even[0], [b_held[bit] for bit in bits])
            b_held.update(zip(bits, near))
            rest_of_rows(b_held, half, rows, swap)
        if s == 3:
            stages[0][0] = (together(own, stages[1][-1][0])[0], 0, 0)
    b_held.update({code | 1: [swap(piece, 1) for piece in b_held[code]] for code in range(0, rows, 2)})
    b_held = [b_held[code] for code in range(rows)]
    acc, readies = None, []
    for i, items in enumerate(stages):
        ahead = [(cols - 1, q) for q in range(per_device)] if i == len(stages) - 1 else []
        acc, *readies = add_panels(sizes, per_list, info, items, b_held, acc, ahead)
    for q, piece in enumerate(even):
        acc = add_ready(sizes, per_list, info, piece, cols - 1, q, readies[q], acc, q == per_device - 1)
    return acc.reshape((1, 1) + acc.shape)


def solution(mesh):
    spec = P("row", "col", None, None, None)
    return jax.shard_map(
        functools.partial(on_device, mesh.shape["col"], mesh.shape["row"]),
        mesh=mesh,
        in_specs=(spec, spec, spec),
        out_specs=spec,
        check_vma=False,
    )
```
